32 devices in a mesh: depth: 4 (over x, core), lat: 8 (over z, y).
Axes of the slice: x: 2, y: 2, z: 4, core: 2. Of those that a mesh axis runs over, the one named last changes fastest.
Arguments:
- temp_old: float32 [32, 8, 256, 128], P('depth', 'lat'), may hold values from 0 to 2.5
- material: int32 [32, 8, 256, 128], P('depth', 'lat'), may hold values from 0 to 7
- conduct_table: float32 [8], replicated, may hold values from 0.3 to 3
- capacity_table: float32 [8], replicated, may hold values from 0.5 to 2
- dyn_power: float32 [4, 8, 256, 128], P('depth', 'lat'), may hold values from 0.2 to 4
- leak_ref: float32 [4, 8, 256, 128], P('depth', 'lat'), may hold values from 0.05 to 1
- die_layer: int32 [4], replicated, may hold values from 0 to 31, as said below
Outputs:
- temp_new: float32 [32, 8, 256, 128], P('depth', 'lat')
- die_power: float32 [4, 8, 256, 128], P('depth', 'lat')
The draws below stay inside these ranges and needn't reach their ends.
Inputs may be any that keep to these rules, and one draw needn't show every extreme that they name: `die_layer`: the 4 entries name different layers of the grid; one die lies on layer 0 and one on the top layer.
All inputs are finite; a program needn't handle non-finite values.
Results may differ from the reference program's by a relative error of at most 0.000059.
Values sent between devices are 32-bit elements; how exact they have to be, the bound alone decides.
A program may use at most 128 MiB of HBM per device.

```python
import math
import jax
import jax.numpy as jnp

BX = 256
BY = 128
GX = 1
DIES = 4
MATS = 8
SWEEPS = 6
TILES = 8
GY = 8
NZ = 32


def draw_die_layer(key, part):
    middle = jax.random.permutation(jax.random.fold_in(key, 11), NZ - 2)[:DIES - 2] + 1
    ends = jnp.array([0, NZ - 1], dtype=jnp.int32)
    layers = jnp.concatenate([ends, middle.astype(jnp.int32)])
    order = jax.random.permutation(jax.random.fold_in(key, 23), DIES)
    return layers[order].astype(jnp.int32)


def via_material(key):
    return jax.random.randint(jax.random.fold_in(key, 5), (), 0, MATS).astype(jnp.int32)


def draw_material(key, part):
    chosen = via_material(key)
    base = jax.random.randint(jax.random.fold_in(key, 7), (NZ, TILES, BX, BY), 0, MATS - 1).astype(jnp.int32)
    base = base + (base >= chosen).astype(jnp.int32)
    column = jax.random.randint(jax.random.fold_in(key, 13), (1, TILES, BX, BY), 0, 8) == 0
    wiring = jax.random.randint(jax.random.fold_in(key, 17), (NZ, 1, BX, 1), 0, 8) == 0
    marked = jnp.logical_or(column, wiring)
    return jnp.where(marked, chosen, base).astype(jnp.int32)


def draw_conduct_table(key, part):
    chosen = via_material(key)
    entries = jnp.arange(MATS, dtype=jnp.int32)
    spread = jax.random.uniform(jax.random.fold_in(key, 31), (MATS,), jnp.float32)
    low_value = 0.3 * jnp.exp(jnp.log(10.0 / 3.0) * spread)
    high_value = 2.4 + 0.6 * spread
    return jnp.where(entries == chosen, high_value, low_value).astype(jnp.float32)


def levels(own_key, extent, split, low, high):
    factor_of, own = 1.0, jax.random.fold_in(own_key, 6)
    for axis_at, parts in split:
        draws = jnp.exp(jax.random.uniform(jax.random.fold_in(own, axis_at), (parts,), jnp.float32, low / len(split), high / len(split)))
        factor_of = factor_of * jnp.repeat(draws, extent[axis_at] // parts).reshape([-1 if axis == axis_at else 1 for axis in range(len(extent))])
    return factor_of


def setup_inputs(seed: int = 0) -> dict:
    streams_of = jax.random.split(jax.random.key(seed), 8)
    return {
        "temp_old": jnp.clip(2.5 * jax.random.uniform(streams_of[0], (NZ, TILES, BX, BY), jnp.float32) ** levels(streams_of[0], (NZ, TILES, BX, BY), ((0, 4), (1, 8)), -0.2, 0.2), 0.0, 2.5),
        "material": draw_material(jax.random.fold_in(streams_of[7], 71), 0),
        "conduct_table": draw_conduct_table(jax.random.fold_in(streams_of[7], 71), 0),
        "capacity_table": jnp.clip(jnp.exp(jax.random.uniform(streams_of[3], (MATS,), jnp.float32, math.log(0.5), math.log(2.0))), 0.5, 2.0),
        "dyn_power": jnp.clip(jnp.exp(math.log(4.0) - 2.9957323 * jax.random.uniform(streams_of[4], (DIES, TILES, BX, BY), jnp.float32) ** levels(streams_of[4], (DIES, TILES, BX, BY), ((0, 4), (1, 8)), -0.2, 0.2)), 0.2, 4.0),
        "leak_ref": jnp.clip(jnp.exp(math.log(1.0) - 2.9957323 * jax.random.uniform(streams_of[5], (DIES, TILES, BX, BY), jnp.float32) ** levels(streams_of[5], (DIES, TILES, BX, BY), ((0, 4), (1, 8)), -0.2, 0.2)), 0.05, 1.0),
        "die_layer": draw_die_layer(jax.random.fold_in(streams_of[7], 71), 0),
    }


COND_SLOPE = 0.15
LEAK_SLOPE = 0.5
SINK_CONDUCT = 2.0


def harmonic(first_side, second_side):
    return 2.0 * first_side * second_side / (first_side + second_side)


def to_grid(tiled):
    leading = tiled.shape[0]
    shaped = tiled.reshape(leading, GX, GY, BX, BY)
    return jnp.transpose(shaped, (0, 1, 3, 2, 4)).reshape(leading, GX * BX, GY * BY)


def to_tiles(grid):
    leading = grid.shape[0]
    shaped = grid.reshape(leading, GX, BX, GY, BY)
    return jnp.transpose(shaped, (0, 1, 3, 2, 4)).reshape(leading, GX * GY, BX, BY)


def reference(temp_old, material, conduct_table, capacity_table, dyn_power, leak_ref, die_layer):
    temp_grid = to_grid(temp_old)
    mat_grid = to_grid(material)
    die_temp = temp_grid[die_layer]
    die_power = to_grid(dyn_power) + to_grid(leak_ref) * jnp.exp(LEAK_SLOPE * die_temp)
    cond = conduct_table[mat_grid] * jnp.exp(-COND_SLOPE * temp_grid)
    heat_cap = capacity_table[mat_grid]
    source = jnp.zeros_like(temp_grid).at[die_layer].set(die_power)
    right_side = heat_cap * temp_grid + source
    along_z = jnp.pad(harmonic(cond[1:], cond[:-1]), ((1, 1), (0, 0), (0, 0)))
    along_x = jnp.pad(harmonic(cond[:, 1:], cond[:, :-1]), ((0, 0), (1, 1), (0, 0)))
    along_y = jnp.pad(harmonic(cond[:, :, 1:], cond[:, :, :-1]), ((0, 0), (0, 0), (1, 1)))
    layers = jnp.arange(NZ)[:, None, None]
    sink = jnp.where(layers == 0, SINK_CONDUCT, 0.0)
    diagonal = heat_cap + (along_z[1:] + along_z[:-1] + along_x[:, 1:] + along_x[:, :-1]
                           + along_y[:, :, 1:] + along_y[:, :, :-1]) + sink
    temp = temp_grid
    for sweep_index in range(SWEEPS):
        padded_z = jnp.pad(temp, ((1, 1), (0, 0), (0, 0)))
        padded_x = jnp.pad(temp, ((0, 0), (1, 1), (0, 0)))
        padded_y = jnp.pad(temp, ((0, 0), (0, 0), (1, 1)))
        coupled = (along_z[1:] * padded_z[2:] + along_z[:-1] * padded_z[:-2]
                   + along_x[:, 1:] * padded_x[:, 2:] + along_x[:, :-1] * padded_x[:, :-2]
                   + along_y[:, :, 1:] * padded_y[:, :, 2:] + along_y[:, :, :-1] * padded_y[:, :, :-2])
        temp = (right_side + coupled) / diagonal
    return to_tiles(temp), to_tiles(die_power)
```

```python
import functools

import jax
import jax.numpy as jnp
from jax import lax
from jax.experimental import pallas as pl
from jax.experimental.pallas import tpu as pltpu
from jax.sharding import PartitionSpec as P

SWEEPS = 6
COND_SLOPE = 0.15
LEAK_SLOPE = 0.5
SINK_CONDUCT = 2.0
PAD = 8
MESH = pl.DeviceIdType.MESH


def inverse(x):
    r = pl.reciprocal(x, approx=True)
    return r * (2.0 - x * r)


def harmonic(a, b):
    return 2.0 * a * b * inverse(a + b)


def lookup(table_ref, bits):
    level = [table_ref[i] for i in range(8)]
    for bit in bits:
        level = [jnp.where(bit, level[2 * i + 1], level[2 * i]) for i in range(len(level) // 2)]
    return level[0]


def kernel(
    n_lat, rows, layers,
    temp_hbm, mat_hbm, cond_tab, cap_tab, dyn_hbm, leak_hbm, die_layer,
    out_hbm, power_hbm,
    T, ZB, ZA, M, MB, MA, C, CB, CA, YS, YL, YR,
    CZM, CZP, CXM, CXP, CYM, CYP, B, DI, GX, DYN, LEAK, PS, PR, PO, PX, PW,
    zsend, zrecv, ysend, yrecv, dsend, drecv, lsem, osem,
):
    me = lax.axis_index("depth")
    lat = lax.axis_index("lat")
    top = layers - 1
    groups = rows // 8
    has_b, has_a = me > 0, me < 3
    has_l, has_r = lat > 0, lat < n_lat - 1
    sib = me + 1 - 2 * lax.rem(me, 2)
    cross = lax.rem(me + 2, 4)
    body = pl.ds(PAD, rows)
    lane = lax.broadcasted_iota(jnp.int32, (8, 128), 1)
    odd = lax.rem(lane, 2) == 1
    half = lane // 2

    zrow = jnp.zeros((PAD, 128), jnp.float32)

    def clear(z, carry):
        for s in range(SWEEPS):
            T[s, z, pl.ds(0, PAD), :] = zrow
            T[s, z, pl.ds(PAD + rows, PAD), :] = zrow
        C[z, pl.ds(0, PAD), :] = zrow
        C[z, pl.ds(PAD + rows, PAD), :] = zrow
        return carry

    lax.fori_loop(0, layers, clear, 0)

    load_t = pltpu.make_async_copy(temp_hbm, T.at[0, :, body], lsem.at[0])
    load_m = pltpu.make_async_copy(mat_hbm, M, lsem.at[1])
    load_d = pltpu.make_async_copy(dyn_hbm.at[0], DYN, lsem.at[2])
    load_l = pltpu.make_async_copy(leak_hbm.at[0], LEAK, lsem.at[3])
    load_t.start()
    load_m.start()
    load_d.start()
    load_l.start()

    barrier = pltpu.get_barrier_semaphore()

    def greet(d, l):
        pl.semaphore_signal(barrier, inc=1, device_id=(d, l), device_id_type=MESH)

    middle = jnp.logical_and(has_b, has_a)
    greet(sib, lat)
    greet(cross, lat)
    pl.when(middle)(lambda: greet(3 - me, lat))
    pl.when(has_l)(lambda: greet(me, lat - 1))
    pl.when(has_r)(lambda: greet(me, lat + 1))

    @pl.when(jnp.logical_not(has_b))
    def _():
        ZB[...] = jnp.zeros_like(ZB)
        CB[...] = jnp.zeros_like(CB)

    @pl.when(jnp.logical_not(has_a))
    def _():
        ZA[...] = jnp.zeros_like(ZA)
        CA[...] = jnp.zeros_like(CA)

    @pl.when(jnp.logical_not(has_l))
    def _():
        YL[...] = jnp.zeros_like(YL)

    @pl.when(jnp.logical_not(has_r))
    def _():
        YR[...] = jnp.zeros_like(YR)

    count = 2 + jnp.where(middle, 1, 0) + jnp.where(has_l, 1, 0) + jnp.where(has_r, 1, 0)
    pl.semaphore_wait(barrier, count)

    def remote(src, dst, ss, rs, d, l):
        return pltpu.make_async_remote_copy(
            src_ref=src, dst_ref=dst, send_sem=ss, recv_sem=rs,
            device_id=(d, l), device_id_type=MESH)

    def z_down(s):
        return remote(T.at[s, 0, body], ZA.at[s], zsend.at[s, 0], zrecv.at[s, 0], me - 1, lat)

    def z_up(s):
        return remote(T.at[s, top, body], ZB.at[s], zsend.at[s, 1], zrecv.at[s, 1], me + 1, lat)

    m_down = remote(M.at[0], MA, zsend.at[SWEEPS, 0], zrecv.at[SWEEPS, 0], me - 1, lat)
    m_up = remote(M.at[top], MB, zsend.at[SWEEPS, 1], zrecv.at[SWEEPS, 1], me + 1, lat)

    def y_part(s, g, first, size):
        part = pl.ds(first, size)
        to_left = remote(YS.at[s, part], YR.at[s, part], ysend.at[s, g, 0], yrecv.at[s, g, 0], me, lat - 1)
        to_right = remote(YS.at[s, part], YL.at[s, part], ysend.at[s, g, 1], yrecv.at[s, g, 1], me, lat + 1)
        return to_left, to_right

    def y_start(*part):
        to_left, to_right = y_part(*part)
        pl.when(has_l)(to_left.start)
        pl.when(has_r)(to_right.start)

    def y_recv(*part):
        to_left, to_right = y_part(*part)
        pl.when(has_r)(to_left.wait_recv)
        pl.when(has_l)(to_right.wait_recv)

    def y_sent(*part):
        to_left, to_right = y_part(*part)
        pl.when(has_l)(to_left.wait_send)
        pl.when(has_r)(to_right.wait_send)

    inner = layers - 2
    first_half = inner // 2
    parts = ((0, 0, 2), (1, 2, first_half), (2, 2 + first_half, inner - first_half))
    whole_part = (0, 0, layers)

    def place(z):
        return jnp.where(z == 0, 0, jnp.where(z == top, 1, z + 1))

    load_t.wait()
    pl.when(has_b)(z_down(0).start)
    pl.when(has_a)(z_up(0).start)
    my_core = lax.rem(me, 2)
    my_chip = me // 2
    base = me * layers

    def picked(die):
        at = die_layer[die] - base
        inside = jnp.logical_and(at >= 0, at < layers)
        flag = jnp.where(inside, 1.0, 0.0)
        return flag * T[0, jnp.clip(at, 0, top), body, :]

    for j in range(2):
        PS[j] = picked(1 - my_core + 2 * j)
    to_sib = remote(PS, PR, dsend.at[0], drecv.at[0], sib, lat)
    to_sib.start()
    for j in range(2):
        PO[j] = picked(my_core + 2 * j)

    load_m.wait()

    def conductivity(mat, temp):
        bits = [(mat & (1 << b)) != 0 for b in range(3)]
        return lookup(cond_tab, bits) * jnp.exp(-COND_SLOPE * temp), bits

    def cells(z, carry):
        packed_t = jnp.zeros((8, 128), jnp.float32)
        packed_c = jnp.zeros((8, 128), jnp.float32)
        for k in range(groups):
            t = T[0, z, pl.ds(PAD + 8 * k, 8), :]
            mat = M[z, pl.ds(8 * k, 8), :]
            c, bits = conductivity(mat, t)
            C[z, pl.ds(PAD + 8 * k, 8), :] = c
            DI[z, pl.ds(8 * k, 8), :] = lookup(cap_tab, bits)
            packed_t = jnp.where(half == k, pltpu.roll(t, 2 * k + 1, 1), packed_t)
            packed_c = jnp.where(half == k, pltpu.roll(c, 2 * k + 1, 1), packed_c)
        YS[0, place(z)] = packed_t
        YS[SWEEPS, place(z)] = packed_c
        return carry

    lax.fori_loop(0, layers // 2, cells, 0)

    to_sib.wait_recv()
    PX[0] = PO[1 - my_chip] + PR[1 - my_chip]
    to_cross = remote(PX.at[0], PX.at[1], dsend.at[1], drecv.at[1], cross, lat)
    to_cross.start()
    pl.when(has_b)(m_down.start)
    pl.when(has_a)(m_up.start)

    lax.fori_loop(layers // 2, layers, cells, 0)
    y_start(SWEEPS, *whole_part)
    y_start(0, *whole_part)
    load_d.wait()
    load_l.wait()

    to_cross.wait_recv()
    for k in range(groups):
        part = pl.ds(8 * k, 8)
        die_temp = PO[my_chip, part, :] + PR[my_chip, part, :] + PX[1, part, :]
        PW[me, part, :] = DYN[part, :] + LEAK[part, :] * jnp.exp(LEAK_SLOPE * die_temp)
    power_cross = remote(PW.at[me], PW.at[me], dsend.at[2], drecv.at[2], cross, lat)
    power_sib = remote(PW.at[me], PW.at[me], dsend.at[3], drecv.at[3], sib, lat)
    power_cross.start()
    power_sib.start()
    power_out = pltpu.make_async_copy(PW.at[me], power_hbm.at[0], lsem.at[4])
    power_out.start()

    @pl.when(has_b)
    def _():
        z_up(0).wait_recv()
        m_up.wait_recv()
        for k in range(groups):
            part = pl.ds(8 * k, 8)
            CB[part, :] = conductivity(MB[part, :], ZB[0, part, :])[0]

    @pl.when(has_a)
    def _():
        z_down(0).wait_recv()
        m_down.wait_recv()
        for k in range(groups):
            part = pl.ds(8 * k, 8)
            CA[part, :] = conductivity(MA[part, :], ZA[0, part, :])[0]

    y_recv(SWEEPS, *whole_part)
    y_recv(0, *whole_part)

    def halo_cols(s, z):
        p = place(z)
        return jnp.where(odd, pltpu.roll(YL[s, p], 1, 1), pltpu.roll(YR[s, p], 127, 1))

    lane0 = lane == 0
    lane_last = lane == 127

    def faces(z, below, above):
        cols = halo_cols(SWEEPS, z)
        sink = jnp.where(base + z == 0, SINK_CONDUCT, 0.0)
        for k in range(groups + 1):
            lo = C[z, pl.ds(PAD + 8 * k - 1, 8), :]
            hi = C[z, pl.ds(PAD + 8 * k, 8), :]
            GX[pl.ds(8 * k, 8), :] = 2.0 * lo * hi * inverse(jnp.maximum(lo + hi, 1e-30))
        for k in range(groups):
            part = pl.ds(8 * k, 8)
            c = C[z, pl.ds(PAD + 8 * k, 8), :]
            gzm = harmonic(c, below(k))
            gzp = harmonic(c, above(k))
            gxm = GX[part, :]
            gxp = GX[pl.ds(8 * k + 1, 8), :]
            h = pltpu.roll(cols, (127 - 2 * k) % 128, 1)
            gym = harmonic(c, jnp.where(lane0, h, pltpu.roll(c, 1, 1)))
            gyp = jnp.where(lane_last, harmonic(c, h), pltpu.roll(gym, 127, 1))
            cap = DI[z, part, :]
            inv = inverse(cap + sink + (gzm + gzp + gxm + gxp + gym + gyp))
            CZM[z, part, :] = gzm * inv
            CZP[z, part, :] = gzp * inv
            CXM[z, part, :] = gxm * inv
            CXP[z, part, :] = gxp * inv
            CYM[z, part, :] = gym * inv
            CYP[z, part, :] = gyp * inv
            DI[z, part, :] = inv
            B[z, part, :] = cap * T[0, z, pl.ds(PAD + 8 * k, 8), :] * inv

    def layer_of(ref, z):
        return lambda k: ref[z, pl.ds(PAD + 8 * k, 8), :]

    def halo_of(ref):
        return lambda k: ref[pl.ds(8 * k, 8), :]

    faces(0, halo_of(CB), layer_of(C, 1))

    def inner_faces(z, carry):
        faces(z, layer_of(C, z - 1), layer_of(C, z + 1))
        return carry

    lax.fori_loop(1, 1 + first_half, inner_faces, 0)
    power_cross.wait_recv()
    forward = remote(PW.at[cross], PW.at[cross], dsend.at[4], drecv.at[4], sib, lat)

    sib_cross = lax.rem(sib + 2, 4)
    forward.start()
    lax.fori_loop(1 + first_half, top, inner_faces, 0)
    faces(top, layer_of(C, top - 1), halo_of(CA))

    power_sib.wait_recv()
    forward.wait_recv()

    def add_source(z, carry):
        which = jnp.int32(0)
        flag = jnp.float32(0.0)
        for d in range(4):
            hit = die_layer[d] == base + z
            which = jnp.where(hit, d, which)
            flag = jnp.where(hit, 1.0, flag)
        for k in range(groups):
            part = pl.ds(8 * k, 8)
            B[z, part, :] = B[z, part, :] + flag * PW[which, part, :] * DI[z, part, :]
        return carry

    lax.fori_loop(0, layers, add_source, 0)

    def relax(s, z, below, above, last):
        cols = halo_cols(s, z)
        packed = jnp.zeros((8, 128), jnp.float32)
        for k in range(groups):
            part = pl.ds(8 * k, 8)
            at = PAD + 8 * k
            t = T[s, z, pl.ds(at, 8), :]
            h = pltpu.roll(cols, (127 - 2 * k) % 128, 1)
            left = jnp.where(lane0, h, pltpu.roll(t, 1, 1))
            right = jnp.where(lane_last, h, pltpu.roll(t, 127, 1))
            new = (B[z, part, :] + CZM[z, part, :] * below(k)) + CZP[z, part, :] * above(k)
            new += CXM[z, part, :] * T[s, z, pl.ds(at - 1, 8), :] + CXP[z, part, :] * T[s, z, pl.ds(at + 1, 8), :]
            new += CYM[z, part, :] * left + CYP[z, part, :] * right
            T[s + 1, z, pl.ds(at, 8), :] = new
            if not last:
                packed = jnp.where(half == k, pltpu.roll(new, 2 * k + 1, 1), packed)
        if not last:
            YS[s + 1, place(z)] = packed

    def out_copy(z):
        return pltpu.make_async_copy(T.at[SWEEPS, z, body], out_hbm.at[z], osem.at[z])

    def step_layers(s, last):
        def t_of(z):
            return lambda k: T[s, z, pl.ds(PAD + 8 * k, 8), :]

        def z_of(ref):
            return lambda k: ref[s, pl.ds(8 * k, 8), :]

        def inner_layer(z, carry):
            relax(s, z, t_of(z - 1), t_of(z + 1), last)
            return carry

        return t_of, z_of, inner_layer

    def sweep(s, last, first):
        t_of, z_of, inner_layer = step_layers(s, last)
        if not first:
            y_recv(s, *parts[0])
            pl.when(has_b)(z_up(s).wait_recv)
        relax(s, 0, z_of(ZB), t_of(1), last)
        if not last:
            pl.when(has_b)(z_down(s + 1).start)
        if not first:
            pl.when(has_a)(z_down(s).wait_recv)
        relax(s, top, t_of(top - 1), z_of(ZA), last)
        if not last:
            pl.when(has_a)(z_up(s + 1).start)
            y_start(s + 1, *parts[0])
        else:
            out_copy(0).start()
            out_copy(top).start()
        for g, lo, size in parts[1:]:
            if not first:
                y_recv(s, g, lo, size)
            if last:
                def with_out(z, carry):
                    inner_layer(z, carry)
                    out_copy(z).start()
                    return carry
                lax.fori_loop(lo - 1, lo - 1 + size, with_out, 0)
            else:
                lax.fori_loop(lo - 1, lo - 1 + size, inner_layer, 0)
                y_start(s + 1, g, lo, size)

    sweep(0, False, True)

    def middle_sweep(s, carry):
        sweep(s, False, False)
        return carry

    lax.fori_loop(1, SWEEPS - 1, middle_sweep, 0)
    sweep(SWEEPS - 1, True, False)

    to_sib.wait_send()
    to_cross.wait_send()
    power_cross.wait_send()
    power_sib.wait_send()
    forward.wait_send()
    pl.when(has_b)(m_down.wait_send)
    pl.when(has_a)(m_up.wait_send)
    y_sent(SWEEPS, *whole_part)
    y_sent(0, *whole_part)
    for s in range(SWEEPS):
        pl.when(has_b)(z_down(s).wait_send)
        pl.when(has_a)(z_up(s).wait_send)
        if s:
            for part in parts:
                y_sent(s, *part)
    power_out.wait()
    for z in range(layers):
        out_copy(z).wait()


def solution(mesh):
    n_lat = mesh.shape["lat"]

    def local(temp_old, material, conduct_table, capacity_table, dyn_power, leak_ref, die_layer):
        layers, _, rows, cols = temp_old.shape
        f32 = jnp.float32
        vm = pltpu.VMEM
        block = (layers, rows, cols)
        face = (rows, cols)
        dma = pltpu.SemaphoreType.DMA
        any_spec = pl.BlockSpec(memory_space=pl.ANY)
        smem = pl.BlockSpec(memory_space=pltpu.SMEM)
        temp, power = pl.pallas_call(
            functools.partial(kernel, n_lat, rows, layers),
            out_shape=(jax.ShapeDtypeStruct(block, f32), jax.ShapeDtypeStruct((1,) + face, f32)),
            in_specs=[any_spec, any_spec, smem, smem, any_spec, any_spec, smem],
            out_specs=(any_spec, any_spec),
            scratch_shapes=[
                vm((SWEEPS + 1, layers, rows + 2 * PAD, cols), f32),
                vm((SWEEPS,) + face, f32), vm((SWEEPS,) + face, f32),
                vm(block, jnp.int32), vm(face, jnp.int32), vm(face, jnp.int32),
                vm((layers, rows + 2 * PAD, cols), f32), vm(face, f32), vm(face, f32),
                vm((SWEEPS + 1, layers, 8, cols), f32),
                vm((SWEEPS + 1, layers, 8, cols), f32),
                vm((SWEEPS + 1, layers, 8, cols), f32),
            ] + [vm(block, f32)] * 8 + [
                vm((rows + 8, cols), f32),
                vm(face, f32), vm(face, f32),
                vm((2,) + face, f32), vm((2,) + face, f32), vm((2,) + face, f32), vm((2,) + face, f32),
                vm((4,) + face, f32),
                dma((SWEEPS + 1, 2)), dma((SWEEPS + 1, 2)),
                dma((SWEEPS + 1, 3, 2)), dma((SWEEPS + 1, 3, 2)),
                dma((5,)), dma((5,)), dma((5,)), dma((layers,)),
            ],
            compiler_params=pltpu.CompilerParams(
                collective_id=0, has_side_effects=True, vmem_limit_bytes=48 * 1024 * 1024),
            cost_estimate=pl.CostEstimate(flops=30_000_000, bytes_accessed=3_600_000, transcendentals=400_000),
        )(
            temp_old.reshape(block), material.reshape(block), conduct_table, capacity_table,
            dyn_power.reshape((1,) + face), leak_ref.reshape((1,) + face), die_layer)
        return temp.reshape(temp_old.shape), power.reshape(dyn_power.shape)

    lateral = P("depth", "lat", None, None)
    return jax.shard_map(
        local,
        mesh=mesh,
        in_specs=(lateral, lateral, P(), P(), lateral, lateral, P()),
        out_specs=(lateral, lateral),
        check_vma=False,
    )
```

```python
import functools

import jax
import jax.numpy as jnp
from jax import lax
from jax.experimental import pallas as pl
from jax.experimental.pallas import tpu as pltpu
from jax.sharding import PartitionSpec as P

SWEEPS = 6
COND_SLOPE = 0.15
LEAK_SLOPE = 0.5
SINK_CONDUCT = 2.0
PAD = 8
MESH = pl.DeviceIdType.MESH


class Later:
    def __init__(self, batch):
        self.batch, self.held, self.rounds = batch, [], 0

    def __call__(self, *stores):
        self.held.extend(stores)
        self.rounds += 1
        if self.rounds % self.batch == 0:
            self.flush()

    def flush(self):
        for ref, at, value in self.held:
            ref[at] = value
        self.held = []


def inverse(x):
    r = pl.reciprocal(x, approx=True)
    return r * (2.0 - x * r)


def harmonic(a, b):
    return 2.0 * a * b * inverse(a + b)


def lookup(table_ref, bits):
    level = [table_ref[i] for i in range(8)]
    for bit in bits:
        level = [jnp.where(bit, level[2 * i + 1], level[2 * i]) for i in range(len(level) // 2)]
    return level[0]


def kernel(
    n_lat, rows, layers,
    temp_hbm, mat_hbm, cond_tab, cap_tab, dyn_hbm, leak_hbm, die_layer,
    out_hbm, power_hbm,
    T, ZB, ZA, M, MB, MA, C, CB, CA, YS, YL, YR,
    CZM, CZP, CXM, CXP, CYM, CYP, B, DI, GX, DYN, LEAK, PS, PR, PO, PX, PW,
    zsend, zrecv, ysend, yrecv, dsend, drecv, lsem, osem,
):
    me = lax.axis_index("depth")
    lat = lax.axis_index("lat")
    top = layers - 1
    groups = rows // 8
    has_b, has_a = me > 0, me < 3
    has_l, has_r = lat > 0, lat < n_lat - 1
    sib = me + 1 - 2 * lax.rem(me, 2)
    cross = lax.rem(me + 2, 4)
    body = pl.ds(PAD, rows)
    lane = lax.broadcasted_iota(jnp.int32, (8, 128), 1)
    odd = lax.rem(lane, 2) == 1
    half = lane // 2

    zrow = jnp.zeros((PAD, 128), jnp.float32)

    def clear(z, carry):
        for s in range(SWEEPS):
            T[s, z, pl.ds(0, PAD), :] = zrow
            T[s, z, pl.ds(PAD + rows, PAD), :] = zrow
        C[z, pl.ds(0, PAD), :] = zrow
        C[z, pl.ds(PAD + rows, PAD), :] = zrow
        return carry

    lax.fori_loop(0, layers, clear, 0)

    load_t = pltpu.make_async_copy(temp_hbm, T.at[0, :, body], lsem.at[0])
    load_m = pltpu.make_async_copy(mat_hbm, M, lsem.at[1])
    load_d = pltpu.make_async_copy(dyn_hbm.at[0], DYN, lsem.at[2])
    load_l = pltpu.make_async_copy(leak_hbm.at[0], LEAK, lsem.at[3])
    load_t.start()
    load_m.start()
    load_d.start()
    load_l.start()

    barrier = pltpu.get_barrier_semaphore()

    def greet(d, l):
        pl.semaphore_signal(barrier, inc=1, device_id=(d, l), device_id_type=MESH)

    middle = jnp.logical_and(has_b, has_a)
    greet(sib, lat)
    greet(cross, lat)
    pl.when(middle)(lambda: greet(3 - me, lat))
    pl.when(has_l)(lambda: greet(me, lat - 1))
    pl.when(has_r)(lambda: greet(me, lat + 1))

    @pl.when(jnp.logical_not(has_b))
    def _():
        ZB[...] = jnp.zeros_like(ZB)
        CB[...] = jnp.zeros_like(CB)

    @pl.when(jnp.logical_not(has_a))
    def _():
        ZA[...] = jnp.zeros_like(ZA)
        CA[...] = jnp.zeros_like(CA)

    @pl.when(jnp.logical_not(has_l))
    def _():
        YL[...] = jnp.zeros_like(YL)

    @pl.when(jnp.logical_not(has_r))
    def _():
        YR[...] = jnp.zeros_like(YR)

    count = 2 + jnp.where(middle, 1, 0) + jnp.where(has_l, 1, 0) + jnp.where(has_r, 1, 0)
    pl.semaphore_wait(barrier, count)

    def remote(src, dst, ss, rs, d, l):
        return pltpu.make_async_remote_copy(
            src_ref=src, dst_ref=dst, send_sem=ss, recv_sem=rs,
            device_id=(d, l), device_id_type=MESH)

    def z_down(s):
        return remote(T.at[s, 0, body], ZA.at[s], zsend.at[s, 0], zrecv.at[s, 0], me - 1, lat)

    def z_up(s):
        return remote(T.at[s, top, body], ZB.at[s], zsend.at[s, 1], zrecv.at[s, 1], me + 1, lat)

    m_down = remote(M.at[0], MA, zsend.at[SWEEPS, 0], zrecv.at[SWEEPS, 0], me - 1, lat)
    m_up = remote(M.at[top], MB, zsend.at[SWEEPS, 1], zrecv.at[SWEEPS, 1], me + 1, lat)

    def y_part(s, g, first, size):
        part = pl.ds(first, size)
        to_left = remote(YS.at[s, part], YR.at[s, part], ysend.at[s, g, 0], yrecv.at[s, g, 0], me, lat - 1)
        to_right = remote(YS.at[s, part], YL.at[s, part], ysend.at[s, g, 1], yrecv.at[s, g, 1], me, lat + 1)
        return to_left, to_right

    def y_start(*part):
        to_left, to_right = y_part(*part)
        pl.when(has_l)(to_left.start)
        pl.when(has_r)(to_right.start)

    def y_recv(*part):
        to_left, to_right = y_part(*part)
        pl.when(has_r)(to_left.wait_recv)
        pl.when(has_l)(to_right.wait_recv)

    def y_sent(*part):
        to_left, to_right = y_part(*part)
        pl.when(has_l)(to_left.wait_send)
        pl.when(has_r)(to_right.wait_send)

    inner = layers - 2
    first_half = inner // 2
    parts = ((0, 0, 2), (1, 2, first_half), (2, 2 + first_half, inner - first_half))
    whole_part = (0, 0, layers)

    def place(z):
        return jnp.where(z == 0, 0, jnp.where(z == top, 1, z + 1))

    load_t.wait()
    pl.when(has_b)(z_down(0).start)
    pl.when(has_a)(z_up(0).start)
    my_core = lax.rem(me, 2)
    my_chip = me // 2
    base = me * layers

    def picked(die):
        at = die_layer[die] - base
        inside = jnp.logical_and(at >= 0, at < layers)
        flag = jnp.where(inside, 1.0, 0.0)
        return flag * T[0, jnp.clip(at, 0, top), body, :]

    for j in range(2):
        PS[j] = picked(1 - my_core + 2 * j)
    to_sib = remote(PS, PR, dsend.at[0], drecv.at[0], sib, lat)
    to_sib.start()
    for j in range(2):
        PO[j] = picked(my_core + 2 * j)

    load_m.wait()

    def conductivity(mat, temp):
        bits = [(mat & (1 << b)) != 0 for b in range(3)]
        return lookup(cond_tab, bits) * jnp.exp(-COND_SLOPE * temp), bits

    def cells(z, carry):
        packed_t = jnp.zeros((8, 128), jnp.float32)
        packed_c = jnp.zeros((8, 128), jnp.float32)
        later = Later(8)
        for k in range(groups):
            t = T[0, z, pl.ds(PAD + 8 * k, 8), :]
            mat = M[z, pl.ds(8 * k, 8), :]
            c, bits = conductivity(mat, t)
            later((C, (z, pl.ds(PAD + 8 * k, 8), slice(None)), c),
                  (DI, (z, pl.ds(8 * k, 8), slice(None)), lookup(cap_tab, bits)))
            packed_t = jnp.where(half == k, pltpu.roll(t, 2 * k + 1, 1), packed_t)
            packed_c = jnp.where(half == k, pltpu.roll(c, 2 * k + 1, 1), packed_c)
        later.flush()
        YS[0, place(z)] = packed_t
        YS[SWEEPS, place(z)] = packed_c
        return carry

    lax.fori_loop(0, layers // 2, cells, 0)

    to_sib.wait_recv()
    PX[0] = PO[1 - my_chip] + PR[1 - my_chip]
    to_cross = remote(PX.at[0], PX.at[1], dsend.at[1], drecv.at[1], cross, lat)
    to_cross.start()
    pl.when(has_b)(m_down.start)
    pl.when(has_a)(m_up.start)

    lax.fori_loop(layers // 2, layers, cells, 0)
    y_start(SWEEPS, *whole_part)
    y_start(0, *whole_part)
    load_d.wait()
    load_l.wait()

    to_cross.wait_recv()
    for k in range(groups):
        part = pl.ds(8 * k, 8)
        die_temp = PO[my_chip, part, :] + PR[my_chip, part, :] + PX[1, part, :]
        PW[me, part, :] = DYN[part, :] + LEAK[part, :] * jnp.exp(LEAK_SLOPE * die_temp)
    power_cross = remote(PW.at[me], PW.at[me], dsend.at[2], drecv.at[2], cross, lat)
    power_sib = remote(PW.at[me], PW.at[me], dsend.at[3], drecv.at[3], sib, lat)
    power_cross.start()
    power_sib.start()
    power_out = pltpu.make_async_copy(PW.at[me], power_hbm.at[0], lsem.at[4])
    power_out.start()

    @pl.when(has_b)
    def _():
        z_up(0).wait_recv()
        m_up.wait_recv()
        for k in range(groups):
            part = pl.ds(8 * k, 8)
            CB[part, :] = conductivity(MB[part, :], ZB[0, part, :])[0]

    @pl.when(has_a)
    def _():
        z_down(0).wait_recv()
        m_down.wait_recv()
        for k in range(groups):
            part = pl.ds(8 * k, 8)
            CA[part, :] = conductivity(MA[part, :], ZA[0, part, :])[0]

    y_recv(SWEEPS, *whole_part)
    y_recv(0, *whole_part)

    def halo_cols(s, z):
        p = place(z)
        return jnp.where(odd, pltpu.roll(YL[s, p], 1, 1), pltpu.roll(YR[s, p], 127, 1))

    lane0 = lane == 0
    lane_last = lane == 127

    def faces(z, below, above):
        cols = halo_cols(SWEEPS, z)
        sink = jnp.where(base + z == 0, SINK_CONDUCT, 0.0)
        later = Later(8)
        for k in range(groups + 1):
            lo = C[z, pl.ds(PAD + 8 * k - 1, 8), :]
            hi = C[z, pl.ds(PAD + 8 * k, 8), :]
            later((GX, (pl.ds(8 * k, 8), slice(None)), 2.0 * lo * hi * inverse(jnp.maximum(lo + hi, 1e-30))))
        later.flush()
        later = Later(4)
        for k in range(groups):
            part = pl.ds(8 * k, 8)
            c = C[z, pl.ds(PAD + 8 * k, 8), :]
            gzm = harmonic(c, below(k))
            gzp = harmonic(c, above(k))
            gxm = GX[part, :]
            gxp = GX[pl.ds(8 * k + 1, 8), :]
            h = pltpu.roll(cols, (127 - 2 * k) % 128, 1)
            gym = harmonic(c, jnp.where(lane0, h, pltpu.roll(c, 1, 1)))
            gyp = jnp.where(lane_last, harmonic(c, h), pltpu.roll(gym, 127, 1))
            cap = DI[z, part, :]
            inv = inverse(cap + sink + (gzm + gzp + gxm + gxp + gym + gyp))
            at = (z, part, slice(None))
            later(
                (CZM, at, gzm * inv), (CZP, at, gzp * inv), (CXM, at, gxm * inv), (CXP, at, gxp * inv),
                (CYM, at, gym * inv), (CYP, at, gyp * inv), (DI, at, inv),
                (B, at, cap * T[0, z, pl.ds(PAD + 8 * k, 8), :] * inv))
        later.flush()

    def layer_of(ref, z):
        return lambda k: ref[z, pl.ds(PAD + 8 * k, 8), :]

    def halo_of(ref):
        return lambda k: ref[pl.ds(8 * k, 8), :]

    faces(0, halo_of(CB), layer_of(C, 1))

    def inner_faces(z, carry):
        faces(z, layer_of(C, z - 1), layer_of(C, z + 1))
        return carry

    lax.fori_loop(1, 1 + first_half, inner_faces, 0)
    power_cross.wait_recv()
    forward = remote(PW.at[cross], PW.at[cross], dsend.at[4], drecv.at[4], sib, lat)

    sib_cross = lax.rem(sib + 2, 4)
    forward.start()
    lax.fori_loop(1 + first_half, top, inner_faces, 0)
    faces(top, layer_of(C, top - 1), halo_of(CA))

    power_sib.wait_recv()
    forward.wait_recv()

    def add_source(z, carry):
        which = jnp.int32(0)
        flag = jnp.float32(0.0)
        for d in range(4):
            hit = die_layer[d] == base + z
            which = jnp.where(hit, d, which)
            flag = jnp.where(hit, 1.0, flag)
        later = Later(8)
        for k in range(groups):
            part = pl.ds(8 * k, 8)
            later((B, (z, part, slice(None)), B[z, part, :] + flag * PW[which, part, :] * DI[z, part, :]))
        later.flush()
        return carry

    lax.fori_loop(0, layers, add_source, 0)

    def relax(s, z, below, above, last):
        cols = halo_cols(s, z)
        packed = jnp.zeros((8, 128), jnp.float32)
        later = Later(16)
        for k in range(groups):
            part = pl.ds(8 * k, 8)
            at = PAD + 8 * k
            t = T[s, z, pl.ds(at, 8), :]
            h = pltpu.roll(cols, (127 - 2 * k) % 128, 1)
            left = jnp.where(lane0, h, pltpu.roll(t, 1, 1))
            right = jnp.where(lane_last, h, pltpu.roll(t, 127, 1))
            new = (B[z, part, :] + CZM[z, part, :] * below(k)) + CZP[z, part, :] * above(k)
            new += CXM[z, part, :] * T[s, z, pl.ds(at - 1, 8), :] + CXP[z, part, :] * T[s, z, pl.ds(at + 1, 8), :]
            new += CYM[z, part, :] * left + CYP[z, part, :] * right
            later((T, (s + 1, z, pl.ds(at, 8), slice(None)), new))
            if not last:
                packed = jnp.where(half == k, pltpu.roll(new, 2 * k + 1, 1), packed)
        later.flush()
        if not last:
            YS[s + 1, place(z)] = packed

    def out_copy(z):
        return pltpu.make_async_copy(T.at[SWEEPS, z, body], out_hbm.at[z], osem.at[z])

    def step_layers(s, last):
        def t_of(z):
            return lambda k: T[s, z, pl.ds(PAD + 8 * k, 8), :]

        def z_of(ref):
            return lambda k: ref[s, pl.ds(8 * k, 8), :]

        def inner_layer(z, carry):
            relax(s, z, t_of(z - 1), t_of(z + 1), last)
            return carry

        return t_of, z_of, inner_layer

    def sweep(s, last, first):
        t_of, z_of, inner_layer = step_layers(s, last)
        if not first:
            y_recv(s, *parts[0])
            pl.when(has_b)(z_up(s).wait_recv)
        relax(s, 0, z_of(ZB), t_of(1), last)
        if not last:
            pl.when(has_b)(z_down(s + 1).start)
        if not first:
            pl.when(has_a)(z_down(s).wait_recv)
        relax(s, top, t_of(top - 1), z_of(ZA), last)
        if not last:
            pl.when(has_a)(z_up(s + 1).start)
            y_start(s + 1, *parts[0])
        else:
            out_copy(0).start()
            out_copy(top).start()
        for g, lo, size in parts[1:]:
            if not first:
                y_recv(s, g, lo, size)
            if last:
                def with_out(z, carry):
                    inner_layer(z, carry)
                    out_copy(z).start()
                    return carry
                lax.fori_loop(lo - 1, lo - 1 + size, with_out, 0)
            else:
                lax.fori_loop(lo - 1, lo - 1 + size, inner_layer, 0)
                y_start(s + 1, g, lo, size)

    sweep(0, False, True)

    def middle_sweep(s, carry):
        sweep(s, False, False)
        return carry

    lax.fori_loop(1, SWEEPS - 1, middle_sweep, 0)
    sweep(SWEEPS - 1, True, False)

    to_sib.wait_send()
    to_cross.wait_send()
    power_cross.wait_send()
    power_sib.wait_send()
    forward.wait_send()
    pl.when(has_b)(m_down.wait_send)
    pl.when(has_a)(m_up.wait_send)
    y_sent(SWEEPS, *whole_part)
    y_sent(0, *whole_part)
    for s in range(SWEEPS):
        pl.when(has_b)(z_down(s).wait_send)
        pl.when(has_a)(z_up(s).wait_send)
        if s:
            for part in parts:
                y_sent(s, *part)
    power_out.wait()
    for z in range(layers):
        out_copy(z).wait()


def solution(mesh):
    n_lat = mesh.shape["lat"]

    def local(temp_old, material, conduct_table, capacity_table, dyn_power, leak_ref, die_layer):
        layers, _, rows, cols = temp_old.shape
        f32 = jnp.float32
        vm = pltpu.VMEM
        block = (layers, rows, cols)
        face = (rows, cols)
        dma = pltpu.SemaphoreType.DMA
        any_spec = pl.BlockSpec(memory_space=pl.ANY)
        smem = pl.BlockSpec(memory_space=pltpu.SMEM)
        temp, power = pl.pallas_call(
            functools.partial(kernel, n_lat, rows, layers),
            out_shape=(jax.ShapeDtypeStruct(block, f32), jax.ShapeDtypeStruct((1,) + face, f32)),
            in_specs=[any_spec, any_spec, smem, smem, any_spec, any_spec, smem],
            out_specs=(any_spec, any_spec),
            scratch_shapes=[
                vm((SWEEPS + 1, layers, rows + 2 * PAD, cols), f32),
                vm((SWEEPS,) + face, f32), vm((SWEEPS,) + face, f32),
                vm(block, jnp.int32), vm(face, jnp.int32), vm(face, jnp.int32),
                vm((layers, rows + 2 * PAD, cols), f32), vm(face, f32), vm(face, f32),
                vm((SWEEPS + 1, layers, 8, cols), f32),
                vm((SWEEPS + 1, layers, 8, cols), f32),
                vm((SWEEPS + 1, layers, 8, cols), f32),
            ] + [vm(block, f32)] * 8 + [
                vm((rows + 8, cols), f32),
                vm(face, f32), vm(face, f32),
                vm((2,) + face, f32), vm((2,) + face, f32), vm((2,) + face, f32), vm((2,) + face, f32),
                vm((4,) + face, f32),
                dma((SWEEPS + 1, 2)), dma((SWEEPS + 1, 2)),
                dma((SWEEPS + 1, 3, 2)), dma((SWEEPS + 1, 3, 2)),
                dma((5,)), dma((5,)), dma((5,)), dma((layers,)),
            ],
            compiler_params=pltpu.CompilerParams(
                collective_id=0, has_side_effects=True, vmem_limit_bytes=62 * 1024 * 1024),
            cost_estimate=pl.CostEstimate(flops=30_000_000, bytes_accessed=3_600_000, transcendentals=400_000),
        )(
            temp_old.reshape(block), material.reshape(block), conduct_table, capacity_table,
            dyn_power.reshape((1,) + face), leak_ref.reshape((1,) + face), die_layer)
        return temp.reshape(temp_old.shape), power.reshape(dyn_power.shape)

    lateral = P("depth", "lat", None, None)
    return jax.shard_map(
        local,
        mesh=mesh,
        in_specs=(lateral, lateral, P(), P(), lateral, lateral, P()),
        out_specs=(lateral, lateral),
        check_vma=False,
    )
```

```python
import functools

import jax
import jax.numpy as jnp
from jax import lax
from jax.experimental import pallas as pl
from jax.experimental.pallas import tpu as pltpu
from jax.sharding import PartitionSpec as P

SWEEPS = 6
COND_SLOPE = 0.15
LEAK_SLOPE = 0.5
SINK_CONDUCT = 2.0
PAD = 8
MESH = pl.DeviceIdType.MESH


class Later:
    def __init__(self, batch):
        self.batch, self.held, self.rounds = batch, [], 0

    def __call__(self, *stores):
        self.held.extend(stores)
        self.rounds += 1
        if self.rounds % self.batch == 0:
            self.flush()

    def flush(self):
        for ref, at, value in self.held:
            ref[at] = value
        self.held = []


def inverse(x):
    r = pl.reciprocal(x, approx=True)
    return r * (2.0 - x * r)


def harmonic(a, b):
    return 2.0 * a * b * inverse(a + b)


def lookup(table_ref, bits):
    level = [table_ref[i] for i in range(8)]
    for bit in bits:
        level = [jnp.where(bit, level[2 * i + 1], level[2 * i]) for i in range(len(level) // 2)]
    return level[0]


def kernel(
    n_lat, rows, layers,
    temp_hbm, mat_hbm, cond_tab, cap_tab, dyn_hbm, leak_hbm, die_layer,
    out_hbm, power_hbm,
    T, ZB, ZA, M, MB, MA, C, CB, CA, YS, YL, YR,
    CZM, CZP, CXM, CXP, CYM, CYP, B, DI, GX, DYN, LEAK, PS, PR, PO, PX, PW,
    zsend, zrecv, ysend, yrecv, dsend, drecv, lsem, osem,
):
    me = lax.axis_index("depth")
    lat = lax.axis_index("lat")
    top = layers - 1
    groups = rows // 8
    has_b, has_a = me > 0, me < 3
    has_l, has_r = lat > 0, lat < n_lat - 1
    sib = me + 1 - 2 * lax.rem(me, 2)
    cross = lax.rem(me + 2, 4)
    body = pl.ds(PAD, rows)
    lane = lax.broadcasted_iota(jnp.int32, (8, 128), 1)
    odd = lax.rem(lane, 2) == 1
    half = lane // 2

    zrow = jnp.zeros((PAD, 128), jnp.float32)

    def clear(z, carry):
        for s in range(SWEEPS):
            T[s, z, pl.ds(0, PAD), :] = zrow
            T[s, z, pl.ds(PAD + rows, PAD), :] = zrow
        C[z, pl.ds(0, PAD), :] = zrow
        C[z, pl.ds(PAD + rows, PAD), :] = zrow
        return carry

    lax.fori_loop(0, layers, clear, 0)

    load_t = pltpu.make_async_copy(temp_hbm, T.at[0, :, body], lsem.at[0])
    load_m = pltpu.make_async_copy(mat_hbm, M, lsem.at[1])
    load_d = pltpu.make_async_copy(dyn_hbm.at[0], DYN, lsem.at[2])
    load_l = pltpu.make_async_copy(leak_hbm.at[0], LEAK, lsem.at[3])
    load_t.start()
    load_m.start()
    load_d.start()
    load_l.start()

    barrier = pltpu.get_barrier_semaphore()

    def greet(d, l):
        pl.semaphore_signal(barrier, inc=1, device_id=(d, l), device_id_type=MESH)

    middle = jnp.logical_and(has_b, has_a)
    greet(sib, lat)
    greet(cross, lat)
    pl.when(middle)(lambda: greet(3 - me, lat))
    pl.when(has_l)(lambda: greet(me, lat - 1))
    pl.when(has_r)(lambda: greet(me, lat + 1))

    @pl.when(jnp.logical_not(has_b))
    def _():
        ZB[...] = jnp.zeros_like(ZB)
        CB[...] = jnp.zeros_like(CB)

    @pl.when(jnp.logical_not(has_a))
    def _():
        ZA[...] = jnp.zeros_like(ZA)
        CA[...] = jnp.zeros_like(CA)

    @pl.when(jnp.logical_not(has_l))
    def _():
        YL[...] = jnp.zeros_like(YL)

    @pl.when(jnp.logical_not(has_r))
    def _():
        YR[...] = jnp.zeros_like(YR)

    count = 2 + jnp.where(middle, 1, 0) + jnp.where(has_l, 1, 0) + jnp.where(has_r, 1, 0)
    pl.semaphore_wait(barrier, count)

    def remote(src, dst, ss, rs, d, l):
        return pltpu.make_async_remote_copy(
            src_ref=src, dst_ref=dst, send_sem=ss, recv_sem=rs,
            device_id=(d, l), device_id_type=MESH)

    def z_down(s):
        return remote(T.at[s, 0, body], ZA.at[s], zsend.at[s, 0], zrecv.at[s, 0], me - 1, lat)

    def z_up(s):
        return remote(T.at[s, top, body], ZB.at[s], zsend.at[s, 1], zrecv.at[s, 1], me + 1, lat)

    m_down = remote(M.at[0], MA, zsend.at[SWEEPS, 0], zrecv.at[SWEEPS, 0], me - 1, lat)
    m_up = remote(M.at[top], MB, zsend.at[SWEEPS, 1], zrecv.at[SWEEPS, 1], me + 1, lat)

    def y_part(s, g, first, size):
        part = pl.ds(first, size)
        to_left = remote(YS.at[s, part], YR.at[s, part], ysend.at[s, g, 0], yrecv.at[s, g, 0], me, lat - 1)
        to_right = remote(YS.at[s, part], YL.at[s, part], ysend.at[s, g, 1], yrecv.at[s, g, 1], me, lat + 1)
        return to_left, to_right

    def y_start(*part):
        to_left, to_right = y_part(*part)
        pl.when(has_l)(to_left.start)
        pl.when(has_r)(to_right.start)

    def y_recv(*part):
        to_left, to_right = y_part(*part)
        pl.when(has_r)(to_left.wait_recv)
        pl.when(has_l)(to_right.wait_recv)

    def y_sent(*part):
        to_left, to_right = y_part(*part)
        pl.when(has_l)(to_left.wait_send)
        pl.when(has_r)(to_right.wait_send)

    inner = layers - 2
    first_half = inner // 2
    parts = ((0, 0, 2), (1, 2, first_half), (2, 2 + first_half, inner - first_half))
    whole_part = (0, 0, layers)

    def place(z):
        return jnp.where(z == 0, 0, jnp.where(z == top, 1, z + 1))

    load_t.wait()
    pl.when(has_b)(z_down(0).start)
    pl.when(has_a)(z_up(0).start)
    my_core = lax.rem(me, 2)
    my_chip = me // 2
    base = me * layers

    def picked(die):
        at = die_layer[die] - base
        inside = jnp.logical_and(at >= 0, at < layers)
        flag = jnp.where(inside, 1.0, 0.0)
        return flag * T[0, jnp.clip(at, 0, top), body, :]

    for j in range(2):
        PS[j] = picked(1 - my_core + 2 * j)
    to_sib = remote(PS, PR, dsend.at[0], drecv.at[0], sib, lat)
    to_sib.start()
    for j in range(2):
        PO[j] = picked(my_core + 2 * j)

    load_m.wait()

    def conductivity(mat, temp):
        bits = [(mat & (1 << b)) != 0 for b in range(3)]
        return lookup(cond_tab, bits) * jnp.exp(-COND_SLOPE * temp), bits

    def cells(z, carry):
        packed_t = jnp.zeros((8, 128), jnp.float32)
        packed_c = jnp.zeros((8, 128), jnp.float32)
        later = Later(8)
        for k in range(groups):
            t = T[0, z, pl.ds(PAD + 8 * k, 8), :]
            mat = M[z, pl.ds(8 * k, 8), :]
            c, bits = conductivity(mat, t)
            later((C, (z, pl.ds(PAD + 8 * k, 8), slice(None)), c),
                  (DI, (z, pl.ds(8 * k, 8), slice(None)), lookup(cap_tab, bits)))
            packed_t = jnp.where(half == k, pltpu.roll(t, 2 * k + 1, 1), packed_t)
            packed_c = jnp.where(half == k, pltpu.roll(c, 2 * k + 1, 1), packed_c)
        later.flush()
        YS[0, place(z)] = packed_t
        YS[SWEEPS, place(z)] = packed_c
        return carry

    lax.fori_loop(0, layers // 2, cells, 0)

    to_sib.wait_recv()
    PX[0] = PO[1 - my_chip] + PR[1 - my_chip]
    to_cross = remote(PX.at[0], PX.at[1], dsend.at[1], drecv.at[1], cross, lat)
    to_cross.start()
    pl.when(has_b)(m_down.start)
    pl.when(has_a)(m_up.start)

    lax.fori_loop(layers // 2, layers, cells, 0)
    y_start(SWEEPS, *whole_part)
    y_start(0, *whole_part)
    load_d.wait()
    load_l.wait()

    to_cross.wait_recv()
    for k in range(groups):
        part = pl.ds(8 * k, 8)
        die_temp = PO[my_chip, part, :] + PR[my_chip, part, :] + PX[1, part, :]
        PW[me, part, :] = DYN[part, :] + LEAK[part, :] * jnp.exp(LEAK_SLOPE * die_temp)
    power_cross = remote(PW.at[me], PW.at[me], dsend.at[2], drecv.at[2], cross, lat)
    power_sib = remote(PW.at[me], PW.at[me], dsend.at[3], drecv.at[3], sib, lat)
    power_cross.start()
    power_sib.start()
    power_out = pltpu.make_async_copy(PW.at[me], power_hbm.at[0], lsem.at[4])
    power_out.start()

    @pl.when(has_b)
    def _():
        z_up(0).wait_recv()
        m_up.wait_recv()
        for k in range(groups):
            part = pl.ds(8 * k, 8)
            CB[part, :] = conductivity(MB[part, :], ZB[0, part, :])[0]

    @pl.when(has_a)
    def _():
        z_down(0).wait_recv()
        m_down.wait_recv()
        for k in range(groups):
            part = pl.ds(8 * k, 8)
            CA[part, :] = conductivity(MA[part, :], ZA[0, part, :])[0]

    y_recv(SWEEPS, *whole_part)
    y_recv(0, *whole_part)

    def halo_cols(s, z):
        p = place(z)
        return jnp.where(odd, pltpu.roll(YL[s, p], 1, 1), pltpu.roll(YR[s, p], 127, 1))

    lane0 = lane == 0
    lane_last = lane == 127

    def faces(z, below, above):
        cols = halo_cols(SWEEPS, z)
        sink = jnp.where(base + z == 0, SINK_CONDUCT, 0.0)
        later = Later(8)
        for k in range(groups + 1):
            lo = C[z, pl.ds(PAD + 8 * k - 1, 8), :]
            hi = C[z, pl.ds(PAD + 8 * k, 8), :]
            later((GX, (pl.ds(8 * k, 8), slice(None)), 2.0 * lo * hi * inverse(jnp.maximum(lo + hi, 1e-30))))
        later.flush()
        later = Later(4)
        for k in range(groups):
            part = pl.ds(8 * k, 8)
            c = C[z, pl.ds(PAD + 8 * k, 8), :]
            gzm = below(k)
            gzp = harmonic(c, above(k))
            gxm = GX[part, :]
            gxp = GX[pl.ds(8 * k + 1, 8), :]
            h = pltpu.roll(cols, (127 - 2 * k) % 128, 1)
            gym = harmonic(c, jnp.where(lane0, h, pltpu.roll(c, 1, 1)))
            gyp = jnp.where(lane_last, harmonic(c, h), pltpu.roll(gym, 127, 1))
            cap = DI[z, part, :]
            inv = inverse(cap + sink + (gzm + gzp + gxm + gxp + gym + gyp))
            at = (z, part, slice(None))
            later(
                (CZM, at, gzm * inv), (CZP, at, gzp * inv), (CXM, at, gxm * inv), (CXP, at, gxp * inv),
                (CB, (part, slice(None)), gzp), (CYM, at, gym * inv), (CYP, at, gyp * inv), (DI, at, inv),
                (B, at, cap * T[0, z, pl.ds(PAD + 8 * k, 8), :] * inv))
        later.flush()

    def layer_of(ref, z):
        return lambda k: ref[z, pl.ds(PAD + 8 * k, 8), :]

    def halo_of(ref):
        return lambda k: ref[pl.ds(8 * k, 8), :]

    faces(0, lambda k: harmonic(C[0, pl.ds(PAD + 8 * k, 8), :], CB[pl.ds(8 * k, 8), :]), layer_of(C, 1))

    def inner_faces(z, carry):
        faces(z, halo_of(CB), layer_of(C, z + 1))
        return carry

    lax.fori_loop(1, 1 + first_half, inner_faces, 0)
    power_cross.wait_recv()
    forward = remote(PW.at[cross], PW.at[cross], dsend.at[4], drecv.at[4], sib, lat)

    sib_cross = lax.rem(sib + 2, 4)
    forward.start()
    lax.fori_loop(1 + first_half, top, inner_faces, 0)
    faces(top, halo_of(CB), halo_of(CA))

    power_sib.wait_recv()
    forward.wait_recv()

    def add_source(z, carry):
        which = jnp.int32(0)
        flag = jnp.float32(0.0)
        for d in range(4):
            hit = die_layer[d] == base + z
            which = jnp.where(hit, d, which)
            flag = jnp.where(hit, 1.0, flag)
        later = Later(8)
        for k in range(groups):
            part = pl.ds(8 * k, 8)
            later((B, (z, part, slice(None)), B[z, part, :] + flag * PW[which, part, :] * DI[z, part, :]))
        later.flush()
        return carry

    lax.fori_loop(0, layers, add_source, 0)

    def relax(s, z, below, above, last):
        cols = halo_cols(s, z)
        packed = jnp.zeros((8, 128), jnp.float32)
        later = Later(16)
        for k in range(groups):
            part = pl.ds(8 * k, 8)
            at = PAD + 8 * k
            t = T[s, z, pl.ds(at, 8), :]
            h = pltpu.roll(cols, (127 - 2 * k) % 128, 1)
            left = jnp.where(lane0, h, pltpu.roll(t, 1, 1))
            right = jnp.where(lane_last, h, pltpu.roll(t, 127, 1))
            new = (B[z, part, :] + CZM[z, part, :] * below(k)) + CZP[z, part, :] * above(k)
            new += CXM[z, part, :] * T[s, z, pl.ds(at - 1, 8), :] + CXP[z, part, :] * T[s, z, pl.ds(at + 1, 8), :]
            new += CYM[z, part, :] * left + CYP[z, part, :] * right
            later((T, (s + 1, z, pl.ds(at, 8), slice(None)), new))
            if not last:
                packed = jnp.where(half == k, pltpu.roll(new, 2 * k + 1, 1), packed)
        later.flush()
        if not last:
            YS[s + 1, place(z)] = packed

    def out_copy(z):
        return pltpu.make_async_copy(T.at[SWEEPS, z, body], out_hbm.at[z], osem.at[z])

    def step_layers(s, last):
        def t_of(z):
            return lambda k: T[s, z, pl.ds(PAD + 8 * k, 8), :]

        def z_of(ref):
            return lambda k: ref[s, pl.ds(8 * k, 8), :]

        def inner_layer(z, carry):
            relax(s, z, t_of(z - 1), t_of(z + 1), last)
            return carry

        return t_of, z_of, inner_layer

    def sweep(s, last, first):
        t_of, z_of, inner_layer = step_layers(s, last)
        if not first:
            y_recv(s, *parts[0])
            pl.when(has_b)(z_up(s).wait_recv)
        relax(s, 0, z_of(ZB), t_of(1), last)
        if not last:
            pl.when(has_b)(z_down(s + 1).start)
        if not first:
            pl.when(has_a)(z_down(s).wait_recv)
        relax(s, top, t_of(top - 1), z_of(ZA), last)
        if not last:
            pl.when(has_a)(z_up(s + 1).start)
            y_start(s + 1, *parts[0])
        else:
            out_copy(0).start()
            out_copy(top).start()
        for g, lo, size in parts[1:]:
            if not first:
                y_recv(s, g, lo, size)
            if last:
                def with_out(z, carry):
                    inner_layer(z, carry)
                    out_copy(z).start()
                    return carry
                lax.fori_loop(lo - 1, lo - 1 + size, with_out, 0)
            else:
                lax.fori_loop(lo - 1, lo - 1 + size, inner_layer, 0)
                y_start(s + 1, g, lo, size)

    sweep(0, False, True)

    def middle_sweep(s, carry):
        sweep(s, False, False)
        return carry

    lax.fori_loop(1, SWEEPS - 1, middle_sweep, 0)
    sweep(SWEEPS - 1, True, False)

    to_sib.wait_send()
    to_cross.wait_send()
    power_cross.wait_send()
    power_sib.wait_send()
    forward.wait_send()
    pl.when(has_b)(m_down.wait_send)
    pl.when(has_a)(m_up.wait_send)
    y_sent(SWEEPS, *whole_part)
    y_sent(0, *whole_part)
    for s in range(SWEEPS):
        pl.when(has_b)(z_down(s).wait_send)
        pl.when(has_a)(z_up(s).wait_send)
        if s:
            for part in parts:
                y_sent(s, *part)
    power_out.wait()
    for z in range(layers):
        out_copy(z).wait()


def solution(mesh):
    n_lat = mesh.shape["lat"]

    def local(temp_old, material, conduct_table, capacity_table, dyn_power, leak_ref, die_layer):
        layers, _, rows, cols = temp_old.shape
        f32 = jnp.float32
        vm = pltpu.VMEM
        block = (layers, rows, cols)
        face = (rows, cols)
        dma = pltpu.SemaphoreType.DMA
        any_spec = pl.BlockSpec(memory_space=pl.ANY)
        smem = pl.BlockSpec(memory_space=pltpu.SMEM)
        temp, power = pl.pallas_call(
            functools.partial(kernel, n_lat, rows, layers),
            out_shape=(jax.ShapeDtypeStruct(block, f32), jax.ShapeDtypeStruct((1,) + face, f32)),
            in_specs=[any_spec, any_spec, smem, smem, any_spec, any_spec, smem],
            out_specs=(any_spec, any_spec),
            scratch_shapes=[
                vm((SWEEPS + 1, layers, rows + 2 * PAD, cols), f32),
                vm((SWEEPS,) + face, f32), vm((SWEEPS,) + face, f32),
                vm(block, jnp.int32), vm(face, jnp.int32), vm(face, jnp.int32),
                vm((layers, rows + 2 * PAD, cols), f32), vm(face, f32), vm(face, f32),
                vm((SWEEPS + 1, layers, 8, cols), f32),
                vm((SWEEPS + 1, layers, 8, cols), f32),
                vm((SWEEPS + 1, layers, 8, cols), f32),
            ] + [vm(block, f32)] * 8 + [
                vm((rows + 8, cols), f32),
                vm(face, f32), vm(face, f32),
                vm((2,) + face, f32), vm((2,) + face, f32), vm((2,) + face, f32), vm((2,) + face, f32),
                vm((4,) + face, f32),
                dma((SWEEPS + 1, 2)), dma((SWEEPS + 1, 2)),
                dma((SWEEPS + 1, 3, 2)), dma((SWEEPS + 1, 3, 2)),
                dma((5,)), dma((5,)), dma((5,)), dma((layers,)),
            ],
            compiler_params=pltpu.CompilerParams(
                collective_id=0, has_side_effects=True, vmem_limit_bytes=62 * 1024 * 1024),
            cost_estimate=pl.CostEstimate(flops=30_000_000, bytes_accessed=3_600_000, transcendentals=400_000),
        )(
            temp_old.reshape(block), material.reshape(block), conduct_table, capacity_table,
            dyn_power.reshape((1,) + face), leak_ref.reshape((1,) + face), die_layer)
        return temp.reshape(temp_old.shape), power.reshape(dyn_power.shape)

    lateral = P("depth", "lat", None, None)
    return jax.shard_map(
        local,
        mesh=mesh,
        in_specs=(lateral, lateral, P(), P(), lateral, lateral, P()),
        out_specs=(lateral, lateral),
        check_vma=False,
    )
```
